32 devices in a mesh: grp: 8 (over y, x, core), dom: 4 (over z).
Axes of the slice: x: 2, y: 2, z: 4, core: 2. Of those that a mesh axis runs over, the one named last changes fastest.
Arguments:
- positions: float32 [5632, 1024], P('grp', 'dom'), may hold values from 0 to 32
- energies: float32 [5632, 1024], P('grp', 'dom'), may hold values from -6 to 6
- bucket: int32 [5632], P('grp'), may hold values from 0 to 2047, as said below
- impedance: float32 [3, 2, 64, 32, 256], P(None, None, 'dom', 'grp'), may hold values from -6 to 6
- history: float32 [2, 2, 64, 32, 256], P(None, None, 'dom', 'grp'), may hold values from -1.8 to 1.8
Outputs:
- positions_out: float32 [5632, 1024], P('grp', 'dom')
- energies_out: float32 [5632, 1024], P('grp', 'dom')
- spectrum: float32 [2, 64, 32, 256], P(None, 'dom', 'grp')
The draws below stay inside these ranges and needn't reach their ends.
Inputs may be any that keep to these rules, and one draw needn't show every extreme that they name: Within one train group no two bunches share a bucket; the first bunch of each group sits in bucket 0 and its last bunch in bucket 2048 - 1.
All inputs are finite; a program needn't handle non-finite values.
Results may differ from the reference program's by a relative error of at most 0.00013.
Values sent between devices are 32-bit elements; how exact they have to be, the bound alone decides.
A program may use at most 64 MiB of HBM per device.

```python
import math
import jax
import jax.numpy as jnp
from jax import lax

BINS = 32
N3 = 256
HIST = 2
BUNCH_GRP = 704
N1 = 64
N2 = 32
M = 524288
BUCK_GRP = 2048
BUNCHES = 5632
PART = 1024
N_GRP = 8


def draw_bucket(key, part):

    def one_group(subkey):
        inner = jax.random.permutation(subkey, BUCK_GRP - 2)[:BUNCH_GRP - 2].astype(jnp.int32) + 1
        first = jnp.zeros((1,), jnp.int32)
        final = jnp.full((1,), BUCK_GRP - 1, jnp.int32)
        return jnp.concatenate([first, inner, final])
    subkeys = jax.random.split(jax.random.fold_in(key, 7), BUNCHES // BUNCH_GRP)
    return jax.vmap(one_group)(subkeys).reshape(-1)


def shard_levels(stream_key, extent, shards, smallest, high):
    def one(dim, shards_of):
        heights = jax.random.uniform(jax.random.fold_in(jax.random.fold_in(stream_key, 6), dim), (shards_of,), jnp.float32, smallest / len(shards), high / len(shards))
        return jnp.repeat(jnp.exp(heights), extent[dim] // shards_of).reshape((-1,) + (1,) * (len(extent) - dim - 1))

    gain = one(*shards[0])
    for cut in shards[1:]:
        gain = gain * one(*cut)
    return gain


def bell_draw(rng, shape, deviation, most, shards=(), kind=jnp.bfloat16):
    values = jax.random.normal(rng, shape, jnp.float32) * deviation
    if len(shards) > 0:
        values = shard_levels(rng, shape, shards, -0.22, 0.18) * values
    return jnp.clip(values, min=-most, max=most).astype(kind)


def setup_inputs(seed: int = 0) -> dict:
    key_of = jax.random.split(jax.random.key(seed), 6)
    return {
        "positions": jnp.clip(32.0 * jax.random.uniform(key_of[0], (BUNCHES, PART), jnp.float32) ** shard_levels(key_of[0], (BUNCHES, PART), ((0, 8), (1, 4)), -0.2, 0.2), 0.0, 32.0),
        "energies": bell_draw(key_of[1], (BUNCHES, PART), 1.0, 6.0, ((0, 8), (1, 4)), jnp.float32),
        "bucket": draw_bucket(jax.random.fold_in(key_of[5], 71), 0),
        "impedance": bell_draw(key_of[3], (HIST + 1, 2, N1, N2, N3), 1.0, 6.0, ((2, 4), (3, 8)), jnp.float32),
        "history": bell_draw(key_of[4], (HIST, 2, N1, N2, N3), 0.3, 1.8, ((2, 4), (3, 8)), jnp.float32),
    }


def kernel_table(places):
    centers = jnp.arange(BINS, dtype=places.dtype) + 0.5
    offset = places[:, None, :] - centers[None, :, None]
    return jnp.exp(-0.5 * offset * offset)

def to_grid(values):
    return values.reshape(N3, N2, N1).transpose(2, 1, 0)

def reference(positions, energies, bucket, impedance, history):
    place_blocks = positions.reshape(BUNCHES // 16, 16, PART)

    def block_profile(place_block):
        return lax.optimization_barrier(jnp.sum(kernel_table(place_block), axis=2)) / PART
    profile = lax.map(block_profile, place_blocks).reshape(BUNCHES, BINS)
    group_of = jnp.arange(BUNCHES, dtype=jnp.int32) // BUNCH_GRP
    cycle_bucket = (group_of * BUCK_GRP + bucket).astype(jnp.int32)
    density = jnp.zeros((BUCK_GRP * N_GRP, BINS), profile.dtype).at[cycle_bucket].add(profile).reshape(-1)
    transform = jnp.fft.fft(density) / math.sqrt(BUNCHES)
    spec_real = to_grid(jnp.real(transform))
    spec_imag = to_grid(jnp.imag(transform))
    spectrum = jnp.stack([spec_real, spec_imag])
    volt_real = impedance[0, 0] * spec_real - impedance[0, 1] * spec_imag
    volt_imag = impedance[0, 0] * spec_imag + impedance[0, 1] * spec_real
    for earlier in range(HIST):
        past_real = history[earlier, 0]
        past_imag = history[earlier, 1]
        volt_real = volt_real + impedance[earlier + 1, 0] * past_real - impedance[earlier + 1, 1] * past_imag
        volt_imag = volt_imag + impedance[earlier + 1, 0] * past_imag + impedance[earlier + 1, 1] * past_real
    induced = volt_real.transpose(2, 1, 0).reshape(-1) + 1j * volt_imag.transpose(2, 1, 0).reshape(-1)
    voltage = jnp.real(jnp.fft.ifft(induced)) * math.sqrt(M)
    volt_rows = voltage.reshape(-1, BINS)[cycle_bucket]

    def kick_block(inputs):
        place_block, volt_block = inputs
        table_block = kernel_table(place_block)
        weighted = jnp.einsum('bjp,bj->bp', table_block, volt_block, precision=lax.Precision.HIGHEST)
        return weighted / lax.optimization_barrier(jnp.sum(table_block, axis=1))
    kick_volts = lax.map(kick_block, (place_blocks, volt_rows.reshape(BUNCHES // 16, 16, BINS))).reshape(BUNCHES, PART)
    energies_out = energies - 0.5 * jnp.sin(2.0 * math.pi * (positions - 0.5 * BINS) / BINS) - kick_volts
    positions_out = positions + 0.25 * energies_out
    return (positions_out, energies_out, spectrum)
```

```python
import functools
import math

import jax
import jax.numpy as jnp
import numpy as np
from jax import lax
from jax.experimental import pallas as pl
from jax.experimental.pallas import tpu as pltpu
from jax.sharding import PartitionSpec as P

BINS = 32
LANES = 128
HIST = 2
MESH = pl.DeviceIdType.MESH
SCALE = math.sqrt(0.5 * math.log2(math.e))
HIGHEST = lax.Precision.HIGHEST
VMEM = pl.BlockSpec(memory_space=pltpu.VMEM)


class Sizes:
    def __init__(self, groups, domains, positions, impedance):
        self.G, self.D = groups, domains
        self.bunches, self.parts = positions.shape
        _, _, self.k1, self.k2, self.n3 = impedance.shape
        self.n1, self.n2 = self.k1 * domains, self.k2 * groups
        self.r1 = self.n1 // groups
        self.cycle = self.n1 * self.n2 * self.n3
        self.naq = self.n3 // domains
        self.mlo = LANES // self.naq
        self.mp = self.n2 // self.mlo
        self.rows = self.mp * self.r1
        self.per_row = self.n3 // BINS
        self.blocks = -(-self.bunches // LANES)
        self.wide = self.blocks * LANES


def tables(z):
    lane = np.arange(LANES)
    na = (np.arange(z.D)[:, None] * z.naq + (lane % z.naq)[None, :]).reshape(-1)
    ml = np.tile(lane // z.naq, z.D)
    key = (na // BINS * z.mlo + ml).astype(np.int32)
    fold = (np.arange(BINS)[:, None] == (na % BINS)[None, :]).astype(np.float32)
    k1 = np.arange(z.n1)
    ang = 2 * np.pi * (k1[:, None] * k1[None, :] % z.n1) / z.n1
    first = np.concatenate([np.cos(ang), -np.sin(ang)], 0)
    m = np.arange(z.mp)[:, None] * z.mlo + (lane // z.naq)[None, :]
    plane = z.n1 * z.n2
    ang = -2 * np.pi * (m[:, None, :] * k1[None, :, None] % plane) / plane
    turn = np.stack([np.cos(ang), np.sin(ang)])
    k2 = np.arange(z.n2)
    ang = -2 * np.pi * (m[None] * k2[:, None, None] % z.n2) / z.n2
    second = np.stack([np.cos(ang), np.sin(ang)])
    k3 = np.arange(z.n3)
    ang = 2 * np.pi * (na[:, None] * k3[None, :] % z.n3) / z.n3
    cos, sin = np.cos(ang), np.sin(ang)
    part = np.tile(lane // z.naq, z.D)[:, None]
    third = np.where(
        part == 0,
        np.concatenate([cos, -sin], 1),
        np.where(part == 1, np.concatenate([sin, cos], 1), 0.0),
    )
    back = np.where(
        part % 2 == 0, np.concatenate([cos, -sin], 1), np.concatenate([sin, cos], 1)
    ).T
    f32 = lambda a: np.asarray(a, np.float32)
    return dict(
        key=key[:, None],
        fold=f32(fold),
        spread=f32(fold.T / (z.parts * z.D)),
        first=f32(first),
        first_t=f32(first.T),
        turn=f32(turn),
        second=f32(second),
        third=f32(third / math.sqrt(z.bunches * z.G)),
        back=f32(back / math.sqrt(z.cycle)),
    )


def split(a):
    hi = a.astype(jnp.bfloat16)
    return hi, (a - hi.astype(jnp.float32)).astype(jnp.bfloat16)


def dot(a, b, dims=((1,), (0,))):
    return lax.dot_general(a, b, (dims, ((), ())), preferred_element_type=jnp.float32)


def dot3(a, b):
    ah, al = split(a)
    bh, bl = split(b)
    return dot(ah, bh) + (dot(ah, bl) + dot(al, bh))


def places(z, bucket):
    nb = bucket // z.per_row
    m = nb % z.n2
    row = m // z.mlo * z.r1 + nb // z.n2
    key = bucket % z.per_row * z.mlo + m % z.mlo
    return row, key


def turned(z, ref, blk):
    n = min(LANES, z.bunches - blk * LANES)
    x = ref[blk * LANES : blk * LANES + n, :]
    if n < LANES:
        x = jnp.concatenate([x, jnp.zeros((LANES - n, x.shape[1]), x.dtype)], 0)
    return x.T


def profile_kernel(z, pos, row, key, lane_key, spread, out, prof):
    for blk in range(z.blocks):
        xs = turned(z, pos, blk) * SCALE
        xs = xs.reshape(z.parts // 8, 8, LANES)
        for j in range(BINS):
            t = xs - (j + 0.5) * SCALE
            s = jnp.sum(jnp.exp2(-(t * t)), axis=0)
            prof[j : j + 1, blk * LANES : (blk + 1) * LANES] = jnp.sum(s, axis=0, keepdims=True)
    ids = lax.broadcasted_iota(jnp.int32, (z.rows, z.wide), 0)
    onehot = (ids == row[...]).astype(jnp.float32).astype(jnp.bfloat16)
    ph, plo = split(prof[...])
    sp = spread[...].astype(jnp.bfloat16)
    for d in range(z.D):
        part = slice(d * LANES, (d + 1) * LANES)
        mine = lane_key[part, :] == key[...]
        high = jnp.where(mine, dot(sp[part], ph), 0.0).astype(jnp.bfloat16)
        low = jnp.where(mine, dot(sp[part], plo), 0.0).astype(jnp.bfloat16)
        line = dot(onehot, high, ((1,), (1,))) + dot(onehot, low, ((1,), (1,)))
        out[d] = line.reshape(z.mp, z.r1, LANES)


def greet(z, over):
    barrier = pltpu.get_barrier_semaphore()
    count = 0
    for axis, n in over:
        me = lax.axis_index(axis)
        for k in range(1, n):
            pl.semaphore_signal(
                barrier, inc=1, device_id={axis: lax.rem(me + k, n)}, device_id_type=MESH
            )
        count += n - 1
    pl.semaphore_wait(barrier, count)


def push(axis, n, src_of, dst_of, send, recv):
    me = lax.axis_index(axis)
    copies = []
    for k in range(1, n):
        to = lax.rem(me + k, n)
        c = pltpu.make_async_remote_copy(
            src_ref=src_of(to),
            dst_ref=dst_of(me, k),
            send_sem=send.at[k - 1],
            recv_sem=recv.at[k - 1],
            device_id={axis: to},
            device_id_type=MESH,
        )
        c.start()
        copies.append(c)
    return copies


def forward_comm(z, parts, out, slots, total, s0, r0, s1, r1):
    greet(z, (("dom", z.D), ("grp", z.G)))
    copies = push("dom", z.D, lambda to: parts.at[to], lambda me, k: slots.at[k - 1], s0, r0)
    acc = parts[lax.axis_index("dom")]
    for k, c in enumerate(copies):
        c.wait_recv()
        acc = acc + slots[k]
    total[...] = acc
    g = lax.axis_index("grp")
    rows = lambda i: pl.ds(pl.multiple_of(i * z.r1, z.r1), z.r1)
    more = push("grp", z.G, lambda to: total, lambda me, k: out.at[:, rows(me), :], s1, r1)
    out[:, rows(g), :] = acc
    for c in copies:
        c.wait_send()
    for c in more:
        c.wait()


def swap_comm(z, parts, out, send, recv):
    greet(z, (("dom", z.D),))
    d = lax.axis_index("dom")
    copies = push("dom", z.D, lambda to: parts.at[to], lambda me, k: out.at[me], send, recv)
    out[d] = parts[d]
    for c in copies:
        c.wait()


def backward_comm(z, volt, out, slots, s0, r0, s1, r1):
    greet(z, (("dom", z.D), ("grp", z.G)))
    rows = lambda i: pl.ds(pl.multiple_of(i * z.r1, z.r1), z.r1)
    copies = push(
        "grp", z.G, lambda to: volt.at[:, rows(to), :], lambda me, k: slots.at[k - 1], s0, r0
    )
    acc = volt[:, rows(lax.axis_index("grp")), :]
    for k, c in enumerate(copies):
        c.wait_recv()
        acc = acc + slots[k]
    d = lax.axis_index("dom")
    out[d] = acc
    more = push("dom", z.D, lambda to: out.at[d], lambda me, k: out.at[me], s1, r1)
    for c in copies:
        c.wait_send()
    for c in more:
        c.wait()


def even_lane(z, shape):
    return lax.broadcasted_iota(jnp.int32, shape, len(shape) - 1) // z.naq % 2 == 0


def forward_kernel(z, x, first, turn, second, out, re, im):
    g = lax.axis_index("grp")
    table = first[...]
    for m in range(z.mp):
        a = dot3(table, x[m])
        ar, ai = a[: z.n1], a[z.n1 :]
        re[m] = ar * turn[0, m] - ai * turn[1, m]
        im[m] = ar * turn[1, m] + ai * turn[0, m]
    even = even_lane(z, (z.n1, LANES))
    for k in range(z.k2):
        k2 = g * z.k2 + k
        yr = yi = 0.0
        for m in range(z.mp):
            cr, ci = second[0, k2, m : m + 1, :], second[1, k2, m : m + 1, :]
            yr = yr + (re[m] * cr - im[m] * ci)
            yi = yi + (re[m] * ci + im[m] * cr)
        s = z.naq
        while s < LANES:
            yr = yr + pltpu.roll(yr, s, 1)
            yi = yi + pltpu.roll(yi, s, 1)
            s *= 2
        out[:, k] = jnp.where(even, yr, yi).reshape(z.D, z.k1, LANES)


def middle_kernel(z, y, imp, hist, third, back, spec, out, volt, cs, sn):
    g, d_own = lax.axis_index("grp"), lax.axis_index("dom")
    n = z.k1 * z.k2
    ids = lax.broadcasted_iota(jnp.int32, (n, LANES), 0)
    lane = lax.broadcasted_iota(jnp.int32, (n, LANES), 1)
    freq = d_own * z.k1 + ids % z.k1 + z.n1 * (g * z.k2 + ids // z.k1)
    even = even_lane(z, (n, LANES))
    total = jnp.zeros((n, 2 * z.n3), jnp.float32)
    for d in range(z.D):
        ang = (freq * (lane % z.naq + d * z.naq) % z.cycle).astype(jnp.float32)
        ang = ang * (2 * math.pi / z.cycle)
        c, s = jnp.cos(ang), jnp.sin(ang)
        s = jnp.where(even, s, -s)
        cs[d], sn[d] = c, s
        p = y[d].reshape(n, LANES)
        p = p * c + pltpu.roll(p, z.naq, 1) * s
        total = total + dot3(p, third[d * LANES : (d + 1) * LANES, :])
    for k in range(z.k2):
        rows = slice(k * z.k1, (k + 1) * z.k1)
        sr, si = total[rows, : z.n3], total[rows, z.n3 :]
        spec[0, :, k, :] = sr
        spec[1, :, k, :] = si
        vr = imp[0, 0, :, k, :] * sr - imp[0, 1, :, k, :] * si
        vi = imp[0, 0, :, k, :] * si + imp[0, 1, :, k, :] * sr
        for h in range(HIST):
            ir, ii = imp[h + 1, 0, :, k, :], imp[h + 1, 1, :, k, :]
            hr, hi = hist[h, 0, :, k, :], hist[h, 1, :, k, :]
            vr = vr + ir * hr - ii * hi
            vi = vi + ir * hi + ii * hr
        volt[rows, : z.n3] = vr
        volt[rows, z.n3 :] = vi
    v = volt[...]
    for d in range(z.D):
        p = dot3(v, back[:, d * LANES : (d + 1) * LANES])
        p = p * cs[d] - pltpu.roll(p, z.naq, 1) * sn[d]
        out[d] = p.reshape(z.k2, z.k1, LANES)


def backward_kernel(z, q, first_t, turn, second, out, re, im):
    g = lax.axis_index("grp")
    even = even_lane(z, (z.n1, LANES))
    for k in range(z.k2):
        p = q[:, k].reshape(z.n1, LANES)
        r = pltpu.roll(p, z.naq, 1)
        re[k] = jnp.where(even, p, r)
        im[k] = jnp.where(even, r, p)
    table = first_t[...]
    for m in range(z.mp):
        ur = ui = 0.0
        for k in range(z.k2):
            k2 = g * z.k2 + k
            cr, ci = second[0, k2, m : m + 1, :], second[1, k2, m : m + 1, :]
            ur = ur + (re[k] * cr + im[k] * ci)
            ui = ui + (im[k] * cr - re[k] * ci)
        tr, ti = turn[0, m], turn[1, m]
        u = jnp.concatenate([ur * tr + ui * ti, ui * tr - ur * ti], 0)
        out[m] = dot3(table, u)


def kick_kernel(z, pos, ener, row, key, lane_key, fold, w, pos_out, ener_out, volts, xt, kt):
    ids = lax.broadcasted_iota(jnp.int32, (z.rows, z.wide), 0)
    onehot = (ids == row[...]).astype(jnp.float32).astype(jnp.bfloat16)
    rows_t = jnp.zeros((BINS, z.wide), jnp.float32)
    fo = fold[...].astype(jnp.bfloat16)
    for d in range(z.D):
        part = slice(d * LANES, (d + 1) * LANES)
        mine = lane_key[part, :] == key[...]
        wh, wl = split(w[d].reshape(z.rows, LANES).T)
        high = jnp.where(mine, dot(wh, onehot), 0.0).astype(jnp.bfloat16)
        low = jnp.where(mine, dot(wl, onehot), 0.0).astype(jnp.bfloat16)
        rows_t = rows_t + (dot(fo[:, part], high) + dot(fo[:, part], low))
    volts[...] = rows_t
    step = 64
    for blk in range(z.blocks):
        n = min(LANES, z.bunches - blk * LANES)
        xt[...] = turned(z, pos, blk) * SCALE

        def some(i, carry):
            at = pl.ds(pl.multiple_of(i * step, step), step)
            xs = xt[at, :]
            num = jnp.zeros((step, LANES), jnp.float32)
            den = jnp.zeros((step, LANES), jnp.float32)
            for j in range(BINS):
                t = xs - (j + 0.5) * SCALE
                e = jnp.exp2(-(t * t))
                num = num + e * volts[j : j + 1, blk * LANES : (blk + 1) * LANES]
                den = den + e
            kt[at, :] = num / den
            return carry

        lax.fori_loop(0, z.parts // step, some, 0)
        rows = slice(blk * LANES, blk * LANES + n)
        x = pos[rows, :]
        turn = jnp.sin((2 * math.pi / BINS) * (x - 0.5 * BINS))
        e = ener[rows, :] - 0.5 * turn - kt[...].T[:n]
        ener_out[rows, :] = e
        pos_out[rows, :] = x + 0.25 * e


def call(body, z, outs, args, scratch=(), collective=None):
    params = dict(vmem_limit_bytes=48 * 2**20)
    if collective is not None:
        params.update(collective_id=collective, has_side_effects=True)
    shapes = [jax.ShapeDtypeStruct(s, jnp.float32) for s in outs]
    return pl.pallas_call(
        functools.partial(body, z),
        out_shape=shapes if len(shapes) > 1 else shapes[0],
        in_specs=[VMEM] * len(args),
        out_specs=[VMEM] * len(shapes) if len(shapes) > 1 else VMEM,
        scratch_shapes=list(scratch),
        compiler_params=pltpu.CompilerParams(**params),
    )(*args)


def on_device(positions, energies, bucket, impedance, history):
    z = Sizes(lax.axis_size("grp"), lax.axis_size("dom"), positions, impedance)
    t = tables(z)
    f32 = lambda *s: pltpu.VMEM(s, jnp.float32)
    dma = lambda n: pltpu.SemaphoreType.DMA((n,))
    row, key = places(z, bucket)
    pad = ((0, 0), (0, z.wide - z.bunches))
    row = jnp.pad(row[None, :], pad, constant_values=-1)
    key = jnp.pad(key[None, :], pad, constant_values=-1)
    slab = (z.mp, z.r1, LANES)
    full = (z.mp, z.n1, LANES)
    chunk = (z.D, z.k2, z.k1, LANES)
    parts = call(
        profile_kernel, z, [(z.D,) + slab],
        (positions, row, key, t["key"], t["spread"]), [f32(BINS, z.wide)],
    )
    x = call(
        forward_comm, z, [full], (parts,),
        [f32(z.D - 1, *slab), f32(*slab), dma(z.D - 1), dma(z.D - 1), dma(z.G - 1), dma(z.G - 1)],
        0,
    )
    y = call(
        forward_kernel, z, [chunk], (x, t["first"], t["turn"], t["second"]),
        [f32(*full), f32(*full)],
    )
    y = call(swap_comm, z, [chunk], (y,), [dma(z.D - 1), dma(z.D - 1)], 1)
    n = z.k1 * z.k2
    spectrum, q = call(
        middle_kernel, z, [(2, z.k1, z.k2, z.n3), chunk],
        (y, impedance, history, t["third"], t["back"]),
        [f32(n, 2 * z.n3), f32(z.D, n, LANES), f32(z.D, n, LANES)],
    )
    q = call(swap_comm, z, [chunk], (q,), [dma(z.D - 1), dma(z.D - 1)], 1)
    volt = call(
        backward_kernel, z, [full], (q, t["first_t"], t["turn"], t["second"]),
        [f32(z.k2, z.n1, LANES), f32(z.k2, z.n1, LANES)],
    )
    w = call(
        backward_comm, z, [(z.D,) + slab], (volt,),
        [f32(z.G - 1, *slab), dma(z.G - 1), dma(z.G - 1), dma(z.D - 1), dma(z.D - 1)],
        2,
    )
    pos_out, ener_out = call(
        kick_kernel, z, [positions.shape, positions.shape],
        (positions, energies, row, key, t["key"], t["fold"], w),
        [f32(BINS, z.wide), f32(z.parts, LANES), f32(z.parts, LANES)],
    )
    return pos_out, ener_out, spectrum


def solution(mesh):
    placed = (
        P("grp", "dom"),
        P("grp", "dom"),
        P("grp"),
        P(None, None, "dom", "grp", None),
        P(None, None, "dom", "grp", None),
    )
    return jax.shard_map(
        on_device,
        mesh=mesh,
        in_specs=placed,
        out_specs=(P("grp", "dom"), P("grp", "dom"), P(None, "dom", "grp", None)),
        check_vma=False,
    )
```

```python
import functools
import math

import jax
import jax.numpy as jnp
import numpy as np
from jax import lax
from jax.experimental import pallas as pl
from jax.experimental.pallas import tpu as pltpu
from jax.sharding import PartitionSpec as P

BINS = 32
LANES = 128
HIST = 2
MESH = pl.DeviceIdType.MESH
SCALE = math.sqrt(0.5 * math.log2(math.e))
HIGHEST = lax.Precision.HIGHEST
VMEM = pl.BlockSpec(memory_space=pltpu.VMEM)


class Sizes:
    def __init__(self, groups, domains, positions, impedance):
        self.G, self.D = groups, domains
        self.bunches, self.parts = positions.shape
        _, _, self.k1, self.k2, self.n3 = impedance.shape
        self.n1, self.n2 = self.k1 * domains, self.k2 * groups
        self.r1 = self.n1 // groups
        self.cycle = self.n1 * self.n2 * self.n3
        self.naq = self.n3 // domains
        self.jb = BINS // domains
        self.mlo = LANES // self.naq
        self.mp = self.n2 // self.mlo
        self.rows = self.mp * self.r1
        self.per_row = self.n3 // BINS
        self.blocks = -(-self.bunches // LANES)
        self.wide = self.blocks * LANES


def tables(z):
    lane = np.arange(LANES)
    q = lane % z.naq
    na = q // z.jb * BINS + np.arange(z.D)[:, None] * z.jb + q % z.jb
    na = na.reshape(-1)
    key = (q // z.jb * z.mlo + lane // z.naq).astype(np.int32)
    k1 = np.arange(z.n1)
    ang = 2 * np.pi * (k1[:, None] * k1[None, :] % z.n1) / z.n1
    first = np.concatenate([np.cos(ang), -np.sin(ang)], 0)
    m = np.arange(z.mp)[:, None] * z.mlo + (lane // z.naq)[None, :]
    plane = z.n1 * z.n2
    ang = -2 * np.pi * (m[:, None, :] * k1[None, :, None] % plane) / plane
    turn = np.stack([np.cos(ang), np.sin(ang)])
    k2 = np.arange(z.n2)
    ang = -2 * np.pi * (m[None] * k2[:, None, None] % z.n2) / z.n2
    second = np.stack([np.cos(ang), np.sin(ang)])
    k3 = np.arange(z.n3)
    ang = 2 * np.pi * (na[:, None] * k3[None, :] % z.n3) / z.n3
    cos, sin = np.cos(ang), np.sin(ang)
    part = np.tile(lane // z.naq, z.D)[:, None]
    third = np.where(
        part == 0,
        np.concatenate([cos, -sin], 1),
        np.where(part == 1, np.concatenate([sin, cos], 1), 0.0),
    )
    back = np.where(
        part % 2 == 0, np.concatenate([cos, -sin], 1), np.concatenate([sin, cos], 1)
    ).T
    f32 = lambda a: np.asarray(a, np.float32)
    return dict(
        key=key[:, None],
        first=f32(first),
        first_t=f32(first.T),
        turn=f32(turn),
        second=f32(second),
        third=f32(third / math.sqrt(z.bunches * z.G)),
        back=f32(back / math.sqrt(z.cycle)),
    )


def split(a):
    hi = a.astype(jnp.bfloat16)
    return hi, (a - hi.astype(jnp.float32)).astype(jnp.bfloat16)


def dot(a, b, dims=((1,), (0,))):
    return lax.dot_general(a, b, (dims, ((), ())), preferred_element_type=jnp.float32)


def dot3(a, b):
    ah, al = split(a)
    bh, bl = split(b)
    return dot(ah, bh) + (dot(ah, bl) + dot(al, bh))


def places(z, bucket):
    nb = bucket // z.per_row
    m = nb % z.n2
    row = m // z.mlo * z.r1 + nb // z.n2
    key = bucket % z.per_row * z.mlo + m % z.mlo
    return row, key


def turned(z, ref, blk):
    n = min(LANES, z.bunches - blk * LANES)
    x = ref[blk * LANES : blk * LANES + n, :]
    if n < LANES:
        x = jnp.concatenate([x, jnp.zeros((LANES - n, x.shape[1]), x.dtype)], 0)
    return x.T


def profile_kernel(z, pos, out):
    for blk in range(z.blocks):
        xs = turned(z, pos, blk) * SCALE
        xs = xs.reshape(z.parts // 8, 8, LANES)
        cols = slice(blk * LANES, (blk + 1) * LANES)
        for j in range(BINS):
            t = xs - (j + 0.5) * SCALE
            s = jnp.sum(jnp.exp2(-(t * t)), axis=0)
            at = slice(j % z.jb, j % z.jb + 1)
            out[j // z.jb, at, cols] = jnp.sum(s, axis=0, keepdims=True)


def found(z, idx, lane_key, g):
    ids = lax.broadcasted_iota(jnp.int32, (z.rows, z.wide), 0)
    onehot = (ids == idx[g, 0:1, :]).astype(jnp.float32).astype(jnp.bfloat16)
    return onehot, lane_key[...] == idx[g, 1:2, :]


def scatter(z, prof, idx, lane_key, x):
    for g in range(z.G):
        onehot, mine = found(z, idx, lane_key, g)
        p = prof[g] * (1.0 / (z.parts * z.D))
        ph = p.astype(jnp.bfloat16).astype(jnp.float32)
        spread = lambda a: jnp.where(mine, jnp.concatenate([a] * (LANES // z.jb), 0), 0.0)
        both = jnp.concatenate([spread(ph), spread(p - ph)], 0).astype(jnp.bfloat16)
        line = dot(onehot, both, ((1,), (1,)))
        line = line[:, :LANES] + line[:, LANES:]
        x[:, g * z.r1 : (g + 1) * z.r1, :] = line.reshape(z.mp, z.r1, LANES)


def gather(z, volt, idx, lane_key, out):
    for g in range(z.G):
        onehot, mine = found(z, idx, lane_key, g)
        w = volt[:, g * z.r1 : (g + 1) * z.r1, :].reshape(z.rows, LANES).T
        both = dot(jnp.concatenate(split(w), 0), onehot)
        both = jnp.where(mine, both[:LANES] + both[LANES:], 0.0)
        out[g] = jnp.sum(both.reshape(LANES // z.jb, z.jb, z.wide), axis=0)


def greet(z, over):
    barrier = pltpu.get_barrier_semaphore()
    count = 0
    for axis, n in over:
        me = lax.axis_index(axis)
        for k in range(1, n):
            pl.semaphore_signal(
                barrier, inc=1, device_id={axis: lax.rem(me + k, n)}, device_id_type=MESH
            )
        count += n - 1
    pl.semaphore_wait(barrier, count)


def push(axis, n, src_of, dst_of, send, recv):
    me = lax.axis_index(axis)
    copies = []
    for k in range(1, n):
        to = lax.rem(me + k, n)
        c = pltpu.make_async_remote_copy(
            src_ref=src_of(to),
            dst_ref=dst_of(me, k),
            send_sem=send.at[k - 1],
            recv_sem=recv.at[k - 1],
            device_id={axis: to},
            device_id_type=MESH,
        )
        c.start()
        copies.append(c)
    return copies


def forward_comm(z, parts, idx, out, idx_out, slots, total, s0, r0, s1, r1, s2, r2):
    greet(z, (("dom", z.D), ("grp", z.G)))
    copies = push("dom", z.D, lambda to: parts.at[to], lambda me, k: slots.at[k - 1], s0, r0)
    copies_i = push("grp", z.G, lambda to: idx, lambda me, k: idx_out.at[me], s2, r2)
    g = lax.axis_index("grp")
    idx_out[g] = idx[...]
    acc = parts[lax.axis_index("dom")]
    for k, c in enumerate(copies):
        c.wait_recv()
        acc = acc + slots[k]
    total[...] = acc
    more = push("grp", z.G, lambda to: total, lambda me, k: out.at[me], s1, r1)
    out[g] = acc
    for c in copies:
        c.wait_send()
    for c in copies_i + more:
        c.wait()


def swap_comm(z, parts, out, send, recv):
    greet(z, (("dom", z.D),))
    d = lax.axis_index("dom")
    copies = push("dom", z.D, lambda to: parts.at[to], lambda me, k: out.at[me], send, recv)
    out[d] = parts[d]
    for c in copies:
        c.wait()


def backward_comm(z, volt, out, slots, s0, r0, s1, r1):
    greet(z, (("dom", z.D), ("grp", z.G)))
    copies = push("grp", z.G, lambda to: volt.at[to], lambda me, k: slots.at[k - 1], s0, r0)
    acc = volt[lax.axis_index("grp")]
    for k, c in enumerate(copies):
        c.wait_recv()
        acc = acc + slots[k]
    d = lax.axis_index("dom")
    out[d] = acc
    more = push("dom", z.D, lambda to: out.at[d], lambda me, k: out.at[me], s1, r1)
    for c in copies:
        c.wait_send()
    for c in more:
        c.wait()


def even_lane(z, shape):
    return lax.broadcasted_iota(jnp.int32, shape, len(shape) - 1) // z.naq % 2 == 0


def forward_kernel(z, prof, idx, lane_key, first, turn, second, out, x, re, im):
    scatter(z, prof, idx, lane_key, x)
    g = lax.axis_index("grp")
    table = first[...]
    for m in range(z.mp):
        a = dot3(table, x[m])
        ar, ai = a[: z.n1], a[z.n1 :]
        re[m] = ar * turn[0, m] - ai * turn[1, m]
        im[m] = ar * turn[1, m] + ai * turn[0, m]
    even = even_lane(z, (z.n1, LANES))
    for k in range(z.k2):
        k2 = g * z.k2 + k
        yr = yi = 0.0
        for m in range(z.mp):
            cr, ci = second[0, k2, m : m + 1, :], second[1, k2, m : m + 1, :]
            yr = yr + (re[m] * cr - im[m] * ci)
            yi = yi + (re[m] * ci + im[m] * cr)
        s = z.naq
        while s < LANES:
            yr = yr + pltpu.roll(yr, s, 1)
            yi = yi + pltpu.roll(yi, s, 1)
            s *= 2
        out[:, k] = jnp.where(even, yr, yi).reshape(z.D, z.k1, LANES)


def middle_kernel(z, y, imp, hist, third, back, spec, out, volt, cs, sn):
    g, d_own = lax.axis_index("grp"), lax.axis_index("dom")
    n = z.k1 * z.k2
    ids = lax.broadcasted_iota(jnp.int32, (n, LANES), 0)
    lane = lax.broadcasted_iota(jnp.int32, (n, LANES), 1)
    freq = d_own * z.k1 + ids % z.k1 + z.n1 * (g * z.k2 + ids // z.k1)
    even = even_lane(z, (n, LANES))
    total = jnp.zeros((n, 2 * z.n3), jnp.float32)
    for d in range(z.D):
        q = lane % z.naq
        na = q // z.jb * BINS + q % z.jb + d * z.jb
        ang = (freq * na % z.cycle).astype(jnp.float32)
        ang = ang * (2 * math.pi / z.cycle)
        c, s = jnp.cos(ang), jnp.sin(ang)
        s = jnp.where(even, s, -s)
        cs[d], sn[d] = c, s
        p = y[d].reshape(n, LANES)
        p = p * c + pltpu.roll(p, z.naq, 1) * s
        total = total + dot3(p, third[d * LANES : (d + 1) * LANES, :])
    for k in range(z.k2):
        rows = slice(k * z.k1, (k + 1) * z.k1)
        sr, si = total[rows, : z.n3], total[rows, z.n3 :]
        spec[0, :, k, :] = sr
        spec[1, :, k, :] = si
        vr = imp[0, 0, :, k, :] * sr - imp[0, 1, :, k, :] * si
        vi = imp[0, 0, :, k, :] * si + imp[0, 1, :, k, :] * sr
        for h in range(HIST):
            ir, ii = imp[h + 1, 0, :, k, :], imp[h + 1, 1, :, k, :]
            hr, hi = hist[h, 0, :, k, :], hist[h, 1, :, k, :]
            vr = vr + ir * hr - ii * hi
            vi = vi + ir * hi + ii * hr
        volt[rows, : z.n3] = vr
        volt[rows, z.n3 :] = vi
    v = volt[...]
    for d in range(z.D):
        p = dot3(v, back[:, d * LANES : (d + 1) * LANES])
        p = p * cs[d] - pltpu.roll(p, z.naq, 1) * sn[d]
        out[d] = p.reshape(z.k2, z.k1, LANES)


def backward_kernel(z, q, idx, lane_key, first_t, turn, second, out, volt, re, im):
    g = lax.axis_index("grp")
    even = even_lane(z, (z.n1, LANES))
    for k in range(z.k2):
        p = q[:, k].reshape(z.n1, LANES)
        r = pltpu.roll(p, z.naq, 1)
        re[k] = jnp.where(even, p, r)
        im[k] = jnp.where(even, r, p)
    table = first_t[...]
    for m in range(z.mp):
        ur = ui = 0.0
        for k in range(z.k2):
            k2 = g * z.k2 + k
            cr, ci = second[0, k2, m : m + 1, :], second[1, k2, m : m + 1, :]
            ur = ur + (re[k] * cr + im[k] * ci)
            ui = ui + (im[k] * cr - re[k] * ci)
        tr, ti = turn[0, m], turn[1, m]
        u = jnp.concatenate([ur * tr + ui * ti, ui * tr - ur * ti], 0)
        volt[m] = dot3(table, u)
    gather(z, volt, idx, lane_key, out)


def kick_kernel(z, pos, ener, w, pos_out, ener_out, xt, kt):
    step = 64
    for blk in range(z.blocks):
        n = min(LANES, z.bunches - blk * LANES)
        xt[...] = turned(z, pos, blk) * SCALE

        def some(i, carry):
            at = pl.ds(pl.multiple_of(i * step, step), step)
            xs = xt[at, :]
            num = jnp.zeros((step, LANES), jnp.float32)
            den = jnp.zeros((step, LANES), jnp.float32)
            for j in range(BINS):
                t = xs - (j + 0.5) * SCALE
                e = jnp.exp2(-(t * t))
                at_j = slice(j % z.jb, j % z.jb + 1)
                num = num + e * w[j // z.jb, at_j, blk * LANES : (blk + 1) * LANES]
                den = den + e
            kt[at, :] = num / den
            return carry

        lax.fori_loop(0, z.parts // step, some, 0)
        rows = slice(blk * LANES, blk * LANES + n)
        x = pos[rows, :]
        turn = jnp.sin((2 * math.pi / BINS) * (x - 0.5 * BINS))
        e = ener[rows, :] - 0.5 * turn - kt[...].T[:n]
        ener_out[rows, :] = e
        pos_out[rows, :] = x + 0.25 * e


def call(body, z, outs, args, scratch=(), collective=None):
    params = dict(vmem_limit_bytes=48 * 2**20)
    if collective is not None:
        params.update(collective_id=collective, has_side_effects=True)
    shapes = [s if hasattr(s, "dtype") else jax.ShapeDtypeStruct(s, jnp.float32) for s in outs]
    return pl.pallas_call(
        functools.partial(body, z),
        out_shape=shapes if len(shapes) > 1 else shapes[0],
        in_specs=[VMEM] * len(args),
        out_specs=[VMEM] * len(shapes) if len(shapes) > 1 else VMEM,
        scratch_shapes=list(scratch),
        compiler_params=pltpu.CompilerParams(**params),
    )(*args)


def on_device(positions, energies, bucket, impedance, history):
    z = Sizes(lax.axis_size("grp"), lax.axis_size("dom"), positions, impedance)
    t = tables(z)
    f32 = lambda *s: pltpu.VMEM(s, jnp.float32)
    dma = lambda n: pltpu.SemaphoreType.DMA((n,))
    row, key = places(z, bucket)
    pad = ((0, 0), (0, z.wide - z.bunches))
    idx = jnp.pad(jnp.stack([row, key]), pad, constant_values=-1)
    lane_key = t["key"]
    full = (z.mp, z.n1, LANES)
    piece = (z.jb, z.wide)
    chunk = (z.D, z.k2, z.k1, LANES)
    parts = call(profile_kernel, z, [(z.D,) + piece], (positions,))
    prof, idx = call(
        forward_comm, z,
        [(z.G,) + piece, jax.ShapeDtypeStruct((z.G,) + idx.shape, jnp.int32)],
        (parts, idx),
        [f32(z.D - 1, *piece), f32(*piece), dma(z.D - 1), dma(z.D - 1)] + [dma(z.G - 1)] * 4,
        0,
    )
    y = call(
        forward_kernel, z, [chunk], (prof, idx, lane_key, t["first"], t["turn"], t["second"]),
        [f32(*full), f32(*full), f32(*full)],
    )
    y = call(swap_comm, z, [chunk], (y,), [dma(z.D - 1), dma(z.D - 1)], 1)
    n = z.k1 * z.k2
    spectrum, q = call(
        middle_kernel, z, [(2, z.k1, z.k2, z.n3), chunk],
        (y, impedance, history, t["third"], t["back"]),
        [f32(n, 2 * z.n3), f32(z.D, n, LANES), f32(z.D, n, LANES)],
    )
    q = call(swap_comm, z, [chunk], (q,), [dma(z.D - 1), dma(z.D - 1)], 1)
    volt = call(
        backward_kernel, z, [(z.G,) + piece], (q, idx, lane_key, t["first_t"], t["turn"], t["second"]),
        [f32(*full), f32(z.k2, z.n1, LANES), f32(z.k2, z.n1, LANES)],
    )
    w = call(
        backward_comm, z, [(z.D,) + piece], (volt,),
        [f32(z.G - 1, *piece), dma(z.G - 1), dma(z.G - 1), dma(z.D - 1), dma(z.D - 1)],
        2,
    )
    pos_out, ener_out = call(
        kick_kernel, z, [positions.shape, positions.shape],
        (positions, energies, w),
        [f32(z.parts, LANES), f32(z.parts, LANES)],
    )
    return pos_out, ener_out, spectrum


def solution(mesh):
    placed = (
        P("grp", "dom"),
        P("grp", "dom"),
        P("grp"),
        P(None, None, "dom", "grp", None),
        P(None, None, "dom", "grp", None),
    )
    return jax.shard_map(
        on_device,
        mesh=mesh,
        in_specs=placed,
        out_specs=(P("grp", "dom"), P("grp", "dom"), P(None, "dom", "grp", None)),
        check_vma=False,
    )
```

```python
import functools
import math

import jax
import jax.numpy as jnp
import numpy as np
from jax import lax
from jax.experimental import pallas as pl
from jax.experimental.pallas import tpu as pltpu
from jax.sharding import PartitionSpec as P

BINS = 32
LANES = 128
HIST = 2
MESH = pl.DeviceIdType.MESH
SCALE = math.sqrt(0.5 * math.log2(math.e))
HIGHEST = lax.Precision.HIGHEST
VMEM = pl.BlockSpec(memory_space=pltpu.VMEM)


class Sizes:
    def __init__(self, groups, domains, positions, impedance):
        self.G, self.D = groups, domains
        self.bunches, self.parts = positions.shape
        _, _, self.k1, self.k2, self.n3 = impedance.shape
        self.n1, self.n2 = self.k1 * domains, self.k2 * groups
        self.r1 = self.n1 // groups
        self.cycle = self.n1 * self.n2 * self.n3
        self.naq = self.n3 // domains
        self.jb = BINS // domains
        self.mlo = LANES // self.naq
        self.mp = self.n2 // self.mlo
        self.rows = self.mp * self.r1
        self.per_row = self.n3 // BINS
        self.blocks = -(-self.bunches // LANES)
        self.wide = self.blocks * LANES


def tables(z):
    lane = np.arange(LANES)
    q = lane % z.naq
    na = q // z.jb * BINS + np.arange(z.D)[:, None] * z.jb + q % z.jb
    na = na.reshape(-1)
    key = (q // z.jb * z.mlo + lane // z.naq).astype(np.int32)
    k1 = np.arange(z.n1)
    ang = 2 * np.pi * (k1[:, None] * k1[None, :] % z.n1) / z.n1
    first = np.concatenate([np.cos(ang), -np.sin(ang)], 0)
    m = np.arange(z.mp)[:, None] * z.mlo + (lane // z.naq)[None, :]
    plane = z.n1 * z.n2
    ang = -2 * np.pi * (m[:, None, :] * k1[None, :, None] % plane) / plane
    turn = np.stack([np.cos(ang), np.sin(ang)])
    k2 = np.arange(z.n2)
    ang = -2 * np.pi * (m[None] * k2[:, None, None] % z.n2) / z.n2
    second = np.stack([np.cos(ang), np.sin(ang)])
    k3 = np.arange(z.n3)
    ang = 2 * np.pi * (na[:, None] * k3[None, :] % z.n3) / z.n3
    cos, sin = np.cos(ang), np.sin(ang)
    part = np.tile(lane // z.naq, z.D)[:, None]
    third = np.where(
        part == 0,
        np.concatenate([cos, -sin], 1),
        np.where(part == 1, np.concatenate([sin, cos], 1), 0.0),
    )
    back = np.where(
        part % 2 == 0, np.concatenate([cos, -sin], 1), np.concatenate([sin, cos], 1)
    ).T
    f32 = lambda a: np.asarray(a, np.float32)
    return dict(
        key=key[:, None],
        first=f32(first),
        first_t=f32(first.T),
        turn=f32(turn),
        second=f32(second),
        third=f32(third / math.sqrt(z.bunches * z.G)),
        back=f32(back / math.sqrt(z.cycle)),
    )


def split(a):
    hi = a.astype(jnp.bfloat16)
    return hi, (a - hi.astype(jnp.float32)).astype(jnp.bfloat16)


def dot(a, b, dims=((1,), (0,))):
    return lax.dot_general(a, b, (dims, ((), ())), preferred_element_type=jnp.float32)


def dot3(a, b):
    ah, al = split(a)
    bh, bl = split(b)
    return dot(ah, bh) + (dot(ah, bl) + dot(al, bh))


def places(z, bucket):
    nb = bucket // z.per_row
    m = nb % z.n2
    row = m // z.mlo * z.r1 + nb // z.n2
    key = bucket % z.per_row * z.mlo + m % z.mlo
    return row, key


def turned(z, ref, blk):
    n = min(LANES, z.bunches - blk * LANES)
    x = ref[blk * LANES : blk * LANES + n, :]
    if n < LANES:
        x = jnp.concatenate([x, jnp.zeros((LANES - n, x.shape[1]), x.dtype)], 0)
    return x.T


def profile_kernel(z, pos, out):
    for blk in range(z.blocks):
        xs = turned(z, pos, blk) * SCALE
        xs = xs.reshape(z.parts // 8, 8, LANES)
        cols = slice(blk * LANES, (blk + 1) * LANES)
        for j in range(BINS):
            t = xs - (j + 0.5) * SCALE
            s = jnp.sum(jnp.exp2(-(t * t)), axis=0)
            at = slice(j % z.jb, j % z.jb + 1)
            out[j // z.jb, at, cols] = jnp.sum(s, axis=0, keepdims=True)


def found(z, idx, lane_key, g):
    ids = lax.broadcasted_iota(jnp.int32, (z.rows, z.wide), 0)
    onehot = (ids == idx[g, 0:1, :]).astype(jnp.float32).astype(jnp.bfloat16)
    return onehot, lane_key[...] == idx[g, 1:2, :]


def scatter(z, prof, idx, lane_key, x):
    for g in range(z.G):
        onehot, mine = found(z, idx, lane_key, g)
        p = prof[g] * (1.0 / (z.parts * z.D))
        ph = p.astype(jnp.bfloat16).astype(jnp.float32)
        spread = lambda a: jnp.where(mine, jnp.concatenate([a] * (LANES // z.jb), 0), 0.0)
        both = jnp.concatenate([spread(ph), spread(p - ph)], 0).astype(jnp.bfloat16)
        line = dot(onehot, both, ((1,), (1,)))
        line = line[:, :LANES] + line[:, LANES:]
        x[:, g * z.r1 : (g + 1) * z.r1, :] = line.reshape(z.mp, z.r1, LANES)


def gather(z, volt, idx, lane_key, out):
    for g in range(z.G):
        onehot, mine = found(z, idx, lane_key, g)
        w = volt[:, g * z.r1 : (g + 1) * z.r1, :].reshape(z.rows, LANES).T
        both = dot(jnp.concatenate(split(w), 0), onehot)
        both = jnp.where(mine, both[:LANES] + both[LANES:], 0.0)
        out[g] = jnp.sum(both.reshape(LANES // z.jb, z.jb, z.wide), axis=0)


def greet(z, over):
    barrier = pltpu.get_barrier_semaphore()
    count = 0
    for axis, n in over:
        me = lax.axis_index(axis)
        for k in range(1, n):
            pl.semaphore_signal(
                barrier, inc=1, device_id={axis: lax.rem(me + k, n)}, device_id_type=MESH
            )
        count += n - 1
    pl.semaphore_wait(barrier, count)


def push(axis, n, src_of, dst_of, send, recv):
    me = lax.axis_index(axis)
    copies = []
    for k in range(1, n):
        to = lax.rem(me + k, n)
        c = pltpu.make_async_remote_copy(
            src_ref=src_of(to),
            dst_ref=dst_of(me, k),
            send_sem=send.at[k - 1],
            recv_sem=recv.at[k - 1],
            device_id={axis: to},
            device_id_type=MESH,
        )
        c.start()
        copies.append(c)
    return copies


def forward_comm(z, parts, idx, out, idx_out, slots, total, s0, r0, s1, r1, s2, r2, meanwhile):
    copies = push("dom", z.D, lambda to: parts.at[to], lambda me, k: slots.at[k - 1], s0, r0)
    copies_i = push("grp", z.G, lambda to: idx, lambda me, k: idx_out.at[me], s2, r2)
    g = lax.axis_index("grp")
    idx_out[g] = idx[...]
    meanwhile()
    acc = parts[lax.axis_index("dom")]
    for k, c in enumerate(copies):
        c.wait_recv()
        acc = acc + slots[k]
    total[...] = acc
    more = push("grp", z.G, lambda to: total, lambda me, k: out.at[me], s1, r1)
    out[g] = acc
    for c in copies:
        c.wait_send()
    for c in copies_i + more:
        c.wait()


def swap_comm(z, parts, out, send, recv):
    d = lax.axis_index("dom")
    copies = push("dom", z.D, lambda to: parts.at[to], lambda me, k: out.at[me], send, recv)
    out[d] = parts[d]
    for c in copies:
        c.wait()


def backward_comm(z, volt, out, slots, s0, r0, s1, r1):
    copies = push("grp", z.G, lambda to: volt.at[to], lambda me, k: slots.at[k - 1], s0, r0)
    acc = volt[lax.axis_index("grp")]
    for k, c in enumerate(copies):
        c.wait_recv()
        acc = acc + slots[k]
    d = lax.axis_index("dom")
    out[d] = acc
    more = push("dom", z.D, lambda to: out.at[d], lambda me, k: out.at[me], s1, r1)
    for c in copies:
        c.wait_send()
    for c in more:
        c.wait()


def even_lane(z, shape):
    return lax.broadcasted_iota(jnp.int32, shape, len(shape) - 1) // z.naq % 2 == 0


def forward_kernel(z, prof, idx, lane_key, first, turn, second, out, x, re, im):
    scatter(z, prof, idx, lane_key, x)
    g = lax.axis_index("grp")
    table = first[...]
    for m in range(z.mp):
        a = dot3(table, x[m])
        ar, ai = a[: z.n1], a[z.n1 :]
        re[m] = ar * turn[0, m] - ai * turn[1, m]
        im[m] = ar * turn[1, m] + ai * turn[0, m]
    even = even_lane(z, (z.n1, LANES))
    for k in range(z.k2):
        k2 = g * z.k2 + k
        yr = yi = 0.0
        for m in range(z.mp):
            cr, ci = second[0, k2, m : m + 1, :], second[1, k2, m : m + 1, :]
            yr = yr + (re[m] * cr - im[m] * ci)
            yi = yi + (re[m] * ci + im[m] * cr)
        s = z.naq
        while s < LANES:
            yr = yr + pltpu.roll(yr, s, 1)
            yi = yi + pltpu.roll(yi, s, 1)
            s *= 2
        out[:, k] = jnp.where(even, yr, yi).reshape(z.D, z.k1, LANES)


def phases(z, cs, sn):
    g, d_own = lax.axis_index("grp"), lax.axis_index("dom")
    n = z.k1 * z.k2
    ids = lax.broadcasted_iota(jnp.int32, (n, LANES), 0)
    lane = lax.broadcasted_iota(jnp.int32, (n, LANES), 1)
    freq = d_own * z.k1 + ids % z.k1 + z.n1 * (g * z.k2 + ids // z.k1)
    even = even_lane(z, (n, LANES))
    q = lane % z.naq
    for d in range(z.D):
        na = q // z.jb * BINS + q % z.jb + d * z.jb
        ang = (freq * na % z.cycle).astype(jnp.float32)
        ang = ang * (2 * math.pi / z.cycle)
        s = jnp.sin(ang)
        cs[d], sn[d] = jnp.cos(ang), jnp.where(even, s, -s)


def middle_kernel(z, y, imp, hist, third, back, spec, out, volt, cs, sn):
    n = z.k1 * z.k2
    total = jnp.zeros((n, 2 * z.n3), jnp.float32)
    for d in range(z.D):
        p = y[d].reshape(n, LANES)
        p = p * cs[d] + pltpu.roll(p, z.naq, 1) * sn[d]
        total = total + dot3(p, third[d * LANES : (d + 1) * LANES, :])
    for k in range(z.k2):
        rows = slice(k * z.k1, (k + 1) * z.k1)
        sr, si = total[rows, : z.n3], total[rows, z.n3 :]
        spec[0, :, k, :] = sr
        spec[1, :, k, :] = si
        vr = imp[0, 0, :, k, :] * sr - imp[0, 1, :, k, :] * si
        vi = imp[0, 0, :, k, :] * si + imp[0, 1, :, k, :] * sr
        for h in range(HIST):
            ir, ii = imp[h + 1, 0, :, k, :], imp[h + 1, 1, :, k, :]
            hr, hi = hist[h, 0, :, k, :], hist[h, 1, :, k, :]
            vr = vr + ir * hr - ii * hi
            vi = vi + ir * hi + ii * hr
        volt[rows, : z.n3] = vr
        volt[rows, z.n3 :] = vi
    v = volt[...]
    for d in range(z.D):
        p = dot3(v, back[:, d * LANES : (d + 1) * LANES])
        p = p * cs[d] - pltpu.roll(p, z.naq, 1) * sn[d]
        out[d] = p.reshape(z.k2, z.k1, LANES)


def backward_kernel(z, q, idx, lane_key, first_t, turn, second, out, volt, re, im):
    g = lax.axis_index("grp")
    even = even_lane(z, (z.n1, LANES))
    for k in range(z.k2):
        p = q[:, k].reshape(z.n1, LANES)
        r = pltpu.roll(p, z.naq, 1)
        re[k] = jnp.where(even, p, r)
        im[k] = jnp.where(even, r, p)
    table = first_t[...]
    for m in range(z.mp):
        ur = ui = 0.0
        for k in range(z.k2):
            k2 = g * z.k2 + k
            cr, ci = second[0, k2, m : m + 1, :], second[1, k2, m : m + 1, :]
            ur = ur + (re[k] * cr + im[k] * ci)
            ui = ui + (im[k] * cr - re[k] * ci)
        tr, ti = turn[0, m], turn[1, m]
        u = jnp.concatenate([ur * tr + ui * ti, ui * tr - ur * ti], 0)
        volt[m] = dot3(table, u)
    gather(z, volt, idx, lane_key, out)


def wake_kernel(
    z, parts, idx, imp, hist, lane_key, first, first_t, turn, second, third, back, spec, out,
    prof, idx_all, slots_d, total, x, re, im, y, y_in, mid, cs, sn, q, q_in, volt, rows, slots_g,
    dom_sems, grp_sems,
):
    greet(z, (("dom", z.D), ("grp", z.G)))
    ds = [dom_sems.at[i] for i in range(8)]
    gs = [grp_sems.at[i] for i in range(6)]
    forward_comm(
        z, parts, idx, prof, idx_all, slots_d, total, ds[0], ds[1], *gs[:4],
        lambda: phases(z, cs, sn),
    )
    forward_kernel(z, prof, idx_all, lane_key, first, turn, second, y, x, re, im)
    swap_comm(z, y, y_in, ds[2], ds[3])
    middle_kernel(z, y_in, imp, hist, third, back, spec, q, mid, cs, sn)
    swap_comm(z, q, q_in, ds[4], ds[5])
    backward_kernel(
        z, q_in, idx_all, lane_key, first_t, turn, second, rows, volt,
        re.at[: z.k2], im.at[: z.k2],
    )
    backward_comm(z, rows, out, slots_g, gs[4], gs[5], ds[6], ds[7])


def kick_kernel(z, pos, ener, w, pos_out, ener_out, xt, kt):
    step = 64
    for blk in range(z.blocks):
        n = min(LANES, z.bunches - blk * LANES)
        xt[...] = turned(z, pos, blk) * SCALE

        def some(i, carry):
            at = pl.ds(pl.multiple_of(i * step, step), step)
            xs = xt[at, :]
            num = jnp.zeros((step, LANES), jnp.float32)
            den = jnp.zeros((step, LANES), jnp.float32)
            for j in range(BINS):
                t = xs - (j + 0.5) * SCALE
                e = jnp.exp2(-(t * t))
                at_j = slice(j % z.jb, j % z.jb + 1)
                num = num + e * w[j // z.jb, at_j, blk * LANES : (blk + 1) * LANES]
                den = den + e
            kt[at, :] = num / den
            return carry

        lax.fori_loop(0, z.parts // step, some, 0)
        rows = slice(blk * LANES, blk * LANES + n)
        x = pos[rows, :]
        turn = jnp.sin((2 * math.pi / BINS) * (x - 0.5 * BINS))
        e = ener[rows, :] - 0.5 * turn - kt[...].T[:n]
        ener_out[rows, :] = e
        pos_out[rows, :] = x + 0.25 * e


def call(body, z, outs, args, scratch=(), collective=None):
    params = dict(vmem_limit_bytes=48 * 2**20)
    if collective is not None:
        params.update(collective_id=collective, has_side_effects=True)
    shapes = [s if hasattr(s, "dtype") else jax.ShapeDtypeStruct(s, jnp.float32) for s in outs]
    return pl.pallas_call(
        functools.partial(body, z),
        out_shape=shapes if len(shapes) > 1 else shapes[0],
        in_specs=[VMEM] * len(args),
        out_specs=[VMEM] * len(shapes) if len(shapes) > 1 else VMEM,
        scratch_shapes=list(scratch),
        compiler_params=pltpu.CompilerParams(**params),
    )(*args)


def on_device(positions, energies, bucket, impedance, history):
    z = Sizes(lax.axis_size("grp"), lax.axis_size("dom"), positions, impedance)
    t = tables(z)
    f32 = lambda *s: pltpu.VMEM(s, jnp.float32)
    row, key = places(z, bucket)
    pad = ((0, 0), (0, z.wide - z.bunches))
    idx = jnp.pad(jnp.stack([row, key]), pad, constant_values=-1)
    lane_key = t["key"]
    full = (z.mp, z.n1, LANES)
    piece = (z.jb, z.wide)
    chunk = (z.D, z.k2, z.k1, LANES)
    parts = call(profile_kernel, z, [(z.D,) + piece], (positions,))
    n = z.k1 * z.k2
    spectrum, w = call(
        wake_kernel, z, [(2, z.k1, z.k2, z.n3), (z.D,) + piece],
        (parts, idx, impedance, history, lane_key, t["first"], t["first_t"], t["turn"],
         t["second"], t["third"], t["back"]),
        [
            f32(z.G, *piece), pltpu.VMEM((z.G,) + idx.shape, jnp.int32),
            f32(z.D - 1, *piece), f32(*piece), f32(*full),
            f32(max(z.mp, z.k2), z.n1, LANES), f32(max(z.mp, z.k2), z.n1, LANES),
            f32(*chunk), f32(*chunk), f32(n, 2 * z.n3), f32(z.D, n, LANES), f32(z.D, n, LANES),
            f32(*chunk), f32(*chunk), f32(*full), f32(z.G, *piece), f32(z.G - 1, *piece),
            pltpu.SemaphoreType.DMA((8, z.D - 1)), pltpu.SemaphoreType.DMA((6, z.G - 1)),
        ],
        0,
    )
    pos_out, ener_out = call(
        kick_kernel, z, [positions.shape, positions.shape],
        (positions, energies, w),
        [f32(z.parts, LANES), f32(z.parts, LANES)],
    )
    return pos_out, ener_out, spectrum


def solution(mesh):
    placed = (
        P("grp", "dom"),
        P("grp", "dom"),
        P("grp"),
        P(None, None, "dom", "grp", None),
        P(None, None, "dom", "grp", None),
    )
    return jax.shard_map(
        on_device,
        mesh=mesh,
        in_specs=placed,
        out_specs=(P("grp", "dom"), P("grp", "dom"), P(None, "dom", "grp", None)),
        check_vma=False,
    )
```
